32 devices in a mesh: ctx: 8 (over z, y), help: 4 (over x, core).
Axes of the slice: x: 2, y: 2, z: 4, core: 2. Of those that a mesh axis runs over, the one named last changes fastest.
Arguments:
- query_rows: bfloat16 [1, 8192, 2048], P(None, ('ctx', 'help')), may hold values from -126 to 126
- key_rows: bfloat16 [1, 8192, 2048], P(None, 'ctx'), may hold values from -6.5 to 6.5
- value_rows: bfloat16 [1, 8192, 2048], P(None, 'ctx'), may hold values from -6 to 6
- output_grad: bfloat16 [1, 8192, 2048], P(None, ('ctx', 'help')), may hold values from -96 to 96
- block_choice: int32 [1, 8192, 2], P(None, ('ctx', 'help')), may hold values from 0 to 7, as said below
Outputs:
- query_grad: bfloat16 [1, 8192, 2048], P(None, ('ctx', 'help'))
- key_grad: bfloat16 [1, 8192, 2048], P(None, ('ctx', 'help'))
- value_grad: bfloat16 [1, 8192, 2048], P(None, ('ctx', 'help'))
The draws below stay inside these ranges and needn't reach their ends.
Inputs may be any that keep to these rules, and one draw needn't show every extreme that they name: `block_choice`: an entry names a block only where it is below the token's own block index; the entries of a token that name blocks name different blocks. In each aligned run of 256 rows of one sequence (the rows of one device) no block is named more than 64 times, and the devices of a sequence's third block name each of its first two blocks exactly 64 times. Blocks early in a sequence are named by the tokens of more blocks than late ones.
All inputs are finite; a program needn't handle non-finite values.
Results may differ from the reference program's by a relative error of at most 0.01.
Values may be sent and summed in bfloat16 or wider, within the bound.
A program may use at most 192 MiB of HBM per device.

```python
import jax
import jax.numpy as jnp
from jax import lax

HEADS = 16
HEAD_DIM = 128
BLOCK = 1024
ROUTED = 2
SEQUENCES = 1
WIDTH = 2048
BLOCKS = 8
SEQ_LEN = 8192
ROWS_DEV = 256
MOST = 64
N_CTX = 8
N_HELP = 4


def base_keys(key):
    drawn = jax.random.normal(jax.random.fold_in(key, 71), (SEQUENCES, SEQ_LEN, WIDTH), jnp.float32)
    return jnp.clip(drawn, -6.0, 6.0)


def draw_key_rows(key, part):
    keys_base = base_keys(key)
    return keys_base.astype(jnp.bfloat16)


def draw_query_rows(key, part):
    values = jnp.clip(jax.random.normal(jax.random.fold_in(key, 73), (SEQUENCES, SEQ_LEN, WIDTH), jnp.float32), -6.0, 6.0)
    return values.astype(jnp.bfloat16)


def draw_block_choice(key, part):
    group_count = SEQ_LEN // ROWS_DEV
    per_route = MOST // 2
    layout = (SEQUENCES, group_count, ROWS_DEV)
    narrow = (SEQUENCES, group_count, 1)
    scores = jax.random.randint(jax.random.fold_in(key, 81), layout, 0, 1 << 20) * ROWS_DEV + jnp.arange(ROWS_DEV, dtype=jnp.int32)
    sort_order = jnp.argsort(scores, axis=2, stable=True)
    rank_of = jnp.argsort(sort_order, axis=2, stable=True).astype(jnp.int32)
    own_block = (jnp.arange(group_count, dtype=jnp.int32) * ROWS_DEV // BLOCK)[None, :, None]
    modulus = jnp.maximum(own_block, 1)
    start_one = jax.random.randint(jax.random.fold_in(key, 82), narrow, 0, 1 << 20) % modulus
    start_two = start_one + 1 + jax.random.randint(jax.random.fold_in(key, 83), narrow, 0, 1 << 20) % jnp.maximum(own_block - 1, 1)
    ceiling = own_block * per_route
    floor_part = ceiling // 2

    def limit_of(salt_value):
        drawn_limit = floor_part + jax.random.randint(jax.random.fold_in(key, salt_value), narrow, 0, 1 << 20) % (ceiling - floor_part + 1)
        return jnp.where(own_block == 2, ceiling, drawn_limit)
    route_one = jnp.where((rank_of < limit_of(84)) & (own_block >= 1), (start_one + rank_of) % modulus, BLOCKS - 1)
    route_two = jnp.where((rank_of < limit_of(85)) & (own_block >= 2), (start_two + rank_of) % modulus, BLOCKS - 1)
    return jnp.stack([route_one, route_two], axis=3).reshape(SEQUENCES, SEQ_LEN, ROUTED).astype(jnp.int32)


def block_levels(stream_key, shape, split, least, largest):
    factor_of = 1.0
    for dim, parts in split:
        steps = jax.random.uniform(jax.random.fold_in(jax.random.fold_in(stream_key, 6), dim), (parts,), jnp.float32, least / len(split), largest / len(split))
        factor_of = factor_of * jnp.repeat(jnp.exp(steps), shape[dim] // parts).reshape((-1,) + (1,) * (len(shape) - 1 - dim))
    return factor_of


def normal_values(stream_key, extent, spread, bound, split=(), kind=jnp.bfloat16):
    gain = block_levels(stream_key, extent, split, -0.22, 0.18) if split else 1.0
    values = jax.random.normal(stream_key, extent, jnp.float32) * spread * gain
    return jnp.minimum(jnp.maximum(values, -bound), bound).astype(kind)


def setup_inputs(seed: int = 0) -> dict:
    streams_of = jax.random.split(jax.random.key(seed), 6)
    query_rows = draw_query_rows(jax.random.fold_in(streams_of[5], 71), 0)
    key_rows = draw_key_rows(jax.random.fold_in(streams_of[5], 71), 0)
    value_rows = normal_values(streams_of[2], (SEQUENCES, SEQ_LEN, WIDTH), 1.0, 6.0, ((1, 8),))
    output_grad = normal_values(streams_of[3], (SEQUENCES, SEQ_LEN, WIDTH), 16.0, 96.0, ((1, 32),))
    block_choice = draw_block_choice(jax.random.fold_in(streams_of[5], 71), 0)
    return {"query_rows": query_rows, "key_rows": key_rows, "value_rows": value_rows, "output_grad": output_grad, "block_choice": block_choice}


NEGATIVE = -1.0e30


def split_heads(matrix):
    return jnp.transpose(matrix.astype(jnp.float32).reshape(matrix.shape[0], HEADS, HEAD_DIM), (1, 0, 2))


def cell_rows(targets, block_id, helper_id):
    positions = jnp.arange(SEQ_LEN, dtype=jnp.int32)
    groups = (positions % BLOCK) // ROWS_DEV
    chosen = jnp.any(targets == block_id, axis=1) & (groups == helper_id)
    routed = jnp.nonzero(chosen, size=N_CTX * MOST, fill_value=SEQ_LEN)[0].astype(jnp.int32)
    own_offsets = jnp.arange(ROWS_DEV, dtype=jnp.int32) + helper_id * ROWS_DEV
    row_ids = jnp.concatenate([block_id * BLOCK + own_offsets, routed])
    limits = jnp.concatenate([own_offsets, jnp.full((N_CTX * MOST,), BLOCK - 1, jnp.int32)])
    return row_ids, limits


def gather_rows(matrix, row_ids):
    present = row_ids < SEQ_LEN
    picked = matrix[jnp.minimum(row_ids, SEQ_LEN - 1)]
    return jnp.where(present[:, None], picked, jnp.zeros_like(picked))


def cell_statistics(query_block, grad_block, key_block, value_block, limits):
    scaling = HEAD_DIM ** -0.5
    allowed = jnp.arange(BLOCK, dtype=jnp.int32)[None, :] <= limits[:, None]
    scores = jnp.einsum("hrd,hkd->hrk", split_heads(query_block), split_heads(key_block)) * scaling
    scores = jnp.where(allowed, scores, NEGATIVE)
    highest = jnp.max(scores, axis=2)
    weights = jnp.where(allowed, jnp.exp(scores - highest[:, :, None]), 0.0)
    products = jnp.einsum("hrd,hkd->hrk", split_heads(grad_block), split_heads(value_block))
    return highest.T, jnp.sum(weights, axis=2).T, jnp.sum(weights * products, axis=2).T


def cell_gradients(query_block, grad_block, key_block, value_block, limits, log_rows, shifts):
    scaling = HEAD_DIM ** -0.5
    allowed = jnp.arange(BLOCK, dtype=jnp.int32)[None, :] <= limits[:, None]
    queries = split_heads(query_block)
    key_heads = split_heads(key_block)
    grads_out = split_heads(grad_block)
    value_heads = split_heads(value_block)
    scores = jnp.einsum("hrd,hkd->hrk", queries, key_heads) * scaling
    probabilities = jnp.where(allowed, jnp.exp(scores - log_rows.T[:, :, None]), 0.0)
    products = jnp.einsum("hrd,hkd->hrk", grads_out, value_heads)
    mixed = probabilities * (products - shifts.T[:, :, None])
    prob_low = lax.optimization_barrier(probabilities.astype(jnp.bfloat16)).astype(jnp.float32)
    mixed_low = lax.optimization_barrier(mixed.astype(jnp.bfloat16)).astype(jnp.float32)
    value_term = jnp.einsum("hrk,hrd->khd", prob_low, grads_out).reshape(BLOCK, WIDTH)
    key_term = jnp.einsum("hrk,hrd->khd", mixed_low, queries).reshape(BLOCK, WIDTH) * scaling
    query_term = jnp.einsum("hrk,hkd->rhd", mixed_low, key_heads).reshape(query_block.shape[0], WIDTH) * scaling
    return query_term, key_term, value_term


def one_sequence(arrays):
    query_rows, key_rows, value_rows, output_grad, block_choice = arrays
    positions = jnp.arange(SEQ_LEN, dtype=jnp.int32)
    own_blocks = (positions // BLOCK)[:, None]
    targets = jnp.where(block_choice < own_blocks, own_blocks - 1 - block_choice, -1).astype(jnp.int32)

    def collect(running, cell_id):
        block_id = cell_id // N_HELP
        helper_id = cell_id % N_HELP
        row_ids, limits = cell_rows(targets, block_id, helper_id)
        key_block = lax.dynamic_slice_in_dim(key_rows, block_id * BLOCK, BLOCK, 0)
        value_block = lax.dynamic_slice_in_dim(value_rows, block_id * BLOCK, BLOCK, 0)
        new_max, new_norm, new_dot = cell_statistics(gather_rows(query_rows, row_ids), gather_rows(output_grad, row_ids), key_block, value_block, limits)
        safe_ids = jnp.minimum(row_ids, SEQ_LEN - 1)
        old_max = running[0][safe_ids]
        old_norm = running[1][safe_ids]
        old_dot = running[2][safe_ids]
        top_value = jnp.maximum(old_max, new_max)
        old_scale = jnp.exp(old_max - top_value)
        new_scale = jnp.exp(new_max - top_value)
        merged = (top_value, old_norm * old_scale + new_norm * new_scale, old_dot * old_scale + new_dot * new_scale)
        updated = tuple(stored.at[row_ids].set(update, mode="drop") for stored, update in zip(running, merged))
        return updated, None

    initial = (jnp.full((SEQ_LEN, HEADS), NEGATIVE, jnp.float32), jnp.zeros((SEQ_LEN, HEADS), jnp.float32), jnp.zeros((SEQ_LEN, HEADS), jnp.float32))
    gathered = lax.scan(collect, initial, jnp.arange(N_CTX * N_HELP, dtype=jnp.int32))[0]
    log_total = gathered[0] + jnp.log(gathered[1])
    centering = gathered[2] / gathered[1]

    def block_pass(query_acc, block_id):
        key_block = lax.dynamic_slice_in_dim(key_rows, block_id * BLOCK, BLOCK, 0)
        value_block = lax.dynamic_slice_in_dim(value_rows, block_id * BLOCK, BLOCK, 0)

        def helper_pass(running, helper_id):
            query_sum, key_acc, value_acc = running
            row_ids, limits = cell_rows(targets, block_id, helper_id)
            present = (row_ids < SEQ_LEN)[:, None]
            safe_ids = jnp.minimum(row_ids, SEQ_LEN - 1)
            log_rows = jnp.where(present, log_total[safe_ids], 0.0)
            shifts = jnp.where(present, centering[safe_ids], 0.0)
            query_term, key_term, value_term = cell_gradients(gather_rows(query_rows, row_ids), gather_rows(output_grad, row_ids), key_block, value_block, limits, log_rows, shifts)
            key_acc = key_acc + lax.optimization_barrier(key_term.astype(jnp.bfloat16)).astype(jnp.float32)
            value_acc = value_acc + lax.optimization_barrier(value_term.astype(jnp.bfloat16)).astype(jnp.float32)
            query_sum = query_sum.at[row_ids].add(query_term, mode="drop")
            return (query_sum, key_acc, value_acc), None

        zeroed = jnp.zeros((BLOCK, WIDTH), jnp.float32)
        result = lax.scan(helper_pass, (query_acc, zeroed, zeroed), jnp.arange(N_HELP, dtype=jnp.int32))[0]
        return result[0], (result[1].astype(jnp.bfloat16), result[2].astype(jnp.bfloat16))

    query_final, block_grads = lax.scan(block_pass, jnp.zeros((SEQ_LEN, WIDTH), jnp.float32), jnp.arange(BLOCKS, dtype=jnp.int32))
    return query_final.astype(jnp.bfloat16), block_grads[0].reshape(SEQ_LEN, WIDTH), block_grads[1].reshape(SEQ_LEN, WIDTH)


def reference(query_rows, key_rows, value_rows, output_grad, block_choice):
    outputs = lax.map(one_sequence, (query_rows, key_rows, value_rows, output_grad, block_choice))
    return (outputs[0], outputs[1], outputs[2])
```

```python
import functools

import jax
import jax.numpy as jnp
from jax import lax
from jax.experimental import pallas as pl
from jax.experimental.pallas import tpu as pltpu
from jax.sharding import PartitionSpec as P

HEAD_DIM = 128
LANES = 128
GROUP_HEADS = 4
NEGATIVE = -1e30
LOG2E = 1.4426950408889634
F32 = jnp.float32
BF16 = jnp.bfloat16


def dot_nt(left, right):
    return lax.dot_general(left, right, (((1,), (1,)), ((), ())), preferred_element_type=F32)


def dot_nn(left, right):
    return lax.dot_general(left, right, (((1,), (0,)), ((), ())), preferred_element_type=F32)


def three_parts(value):
    high = value.astype(BF16).astype(F32)
    rest = value - high
    middle = rest.astype(BF16).astype(F32)
    return jnp.concatenate([high, middle, rest - middle], axis=0).astype(BF16)


def add_parts(value, count):
    return value[:count] + value[count : 2 * count] + value[2 * count :]


def kernel(
    blocks,
    helpers,
    q_ref,
    k_ref,
    v_ref,
    do_ref,
    pick_slots,
    pick_rows,
    select_ref,
    present_ref,
    dq_out,
    dk_out,
    dv_out,
    send_buf,
    recv_buf,
    own_stat,
    stat_blk,
    back_buf,
    log_send,
    log_recv,
    fin_own,
    slot_stat,
    dq_own,
    ret_send,
    ret_recv,
    kv_part,
    sib_recv,
    pair_send,
    pair_recv,
    fwd_s,
    fwd_r,
    stat_s,
    stat_r,
    log_s,
    log_r,
    ret_s,
    ret_r,
    sib_s,
    sib_r,
    pair_s,
    pair_r,
):
    me = lax.axis_index("ctx")
    helper = lax.axis_index("help")
    core = lax.rem(helper, 2)
    xpos = lax.div(helper, 2)
    nx = helpers // 2
    groups = send_buf.shape[0]
    cap = send_buf.shape[3]
    width = send_buf.shape[4]
    heads = width // HEAD_DIM
    rows = q_ref.shape[0]
    keys = k_ref.shape[0]
    slots = blocks * cap
    per_blk = LANES // cap
    tile = 2 * LANES
    tiles = slots // tile
    scaling = HEAD_DIM**-0.5
    scale2 = scaling * LOG2E

    def fwd_copy(g, src, dst):
        return pltpu.make_async_remote_copy(
            send_buf.at[g, dst], recv_buf.at[g, src], fwd_s.at[g, dst], fwd_r.at[g, src],
            device_id={"ctx": dst}, device_id_type=pl.DeviceIdType.MESH,
        )

    def stat_copy(g, src, dst):
        return pltpu.make_async_remote_copy(
            stat_blk.at[g, lax.div(dst, per_blk)], back_buf.at[g, src], stat_s.at[g, dst], stat_r.at[g, src],
            device_id={"ctx": dst}, device_id_type=pl.DeviceIdType.MESH,
        )

    def log_copy(g, src, dst):
        return pltpu.make_async_remote_copy(
            log_send.at[g, dst], log_recv.at[g, src], log_s.at[g, dst], log_r.at[g, src],
            device_id={"ctx": dst}, device_id_type=pl.DeviceIdType.MESH,
        )

    def ret_copy(g, src, dst):
        return pltpu.make_async_remote_copy(
            ret_send.at[g, dst], ret_recv.at[g, src], ret_s.at[g, dst], ret_r.at[g, src],
            device_id={"ctx": dst}, device_id_type=pl.DeviceIdType.MESH,
        )

    def sib_copy(g):
        return pltpu.make_async_remote_copy(
            kv_part.at[g, :, :, 1 - core], sib_recv.at[g], sib_s.at[g], sib_r.at[g],
            device_id={"help": xpos * 2 + 1 - core}, device_id_type=pl.DeviceIdType.MESH,
        )

    def pair_copy(g, src, dst):
        return pltpu.make_async_remote_copy(
            pair_send.at[g, dst], pair_recv.at[g, src], pair_s.at[g, dst], pair_r.at[g, src],
            device_id={"help": dst * 2 + core}, device_id_type=pl.DeviceIdType.MESH,
        )

    def lower(body):
        lax.fori_loop(0, me, lambda i, c: (body(me - 1 - i), c)[1], 0)

    def upper(body):
        lax.fori_loop(me + 1, blocks, lambda i, c: (body(i), c)[1], 0)

    barrier = pltpu.get_barrier_semaphore()

    def greet_ctx(d):
        pl.semaphore_signal(barrier, inc=1, device_id={"ctx": d}, device_id_type=pl.DeviceIdType.MESH)

    lower(greet_ctx)
    upper(greet_ctx)
    pl.semaphore_signal(
        barrier, inc=1, device_id={"help": xpos * 2 + 1 - core}, device_id_type=pl.DeviceIdType.MESH
    )
    for o in range(1, nx):
        pl.semaphore_signal(
            barrier, inc=1, device_id={"help": lax.rem(xpos + o, nx) * 2 + core},
            device_id_type=pl.DeviceIdType.MESH,
        )
    pl.semaphore_wait(barrier, blocks - 1 + nx)

    def pack(g, carry):
        cols = pl.ds(pl.multiple_of(g * width, width), width)
        for which, ref in ((0, q_ref), (1, do_ref)):
            packed = dot_nn(pick_slots[...], ref[:, cols]).astype(BF16)
            send_buf[g, :, which] = packed.reshape(blocks, cap, width)
        lower(lambda d: fwd_copy(g, me, d).start())
        return carry

    lax.fori_loop(0, groups, pack, 0)

    def clear(d, carry):
        @pl.when(d <= me)
        def _():
            def each(g, c):
                recv_buf[g, d] = jnp.zeros(recv_buf.shape[2:], BF16)
                log_recv[g, d] = jnp.zeros(log_recv.shape[2:], F32)
                return c

            lax.fori_loop(0, groups, each, 0)

        @pl.when(d >= me)
        def _():
            def each(g, c):
                back_buf[g, d] = jnp.zeros(back_buf.shape[2:], F32)
                ret_recv[g, d] = jnp.zeros(ret_recv.shape[2:], BF16)
                return c

            lax.fori_loop(0, groups, each, 0)

        return carry

    lax.fori_loop(0, blocks, clear, 0)

    def own_mask():
        row_at = helper * rows + lax.broadcasted_iota(jnp.int32, (keys, rows), 1)
        return lax.broadcasted_iota(jnp.int32, (keys, rows), 0) <= row_at

    def columns(g, h):
        return pl.ds(pl.multiple_of(g * width + h * HEAD_DIM, HEAD_DIM), HEAD_DIM)

    def inner(h):
        return pl.ds(pl.multiple_of(h * HEAD_DIM, HEAD_DIM), HEAD_DIM)

    per_tile = tile // cap

    def routed(g, j, which, h):
        return recv_buf[g, j * per_tile : (j + 1) * per_tile, which, :, inner(h)].reshape(tile, HEAD_DIM)

    def statistics(g):
        upper(lambda s: fwd_copy(g, s, me).wait_recv())

        def head(h, carry):
            key = k_ref[:, columns(g, h)]
            value = v_ref[:, columns(g, h)]

            def local(query, grad, mask):
                scores = dot_nt(key, query) * scale2
                if mask:
                    scores = jnp.where(own_mask(), scores, NEGATIVE)
                top = jnp.max(scores, axis=0, keepdims=True)
                weights = jnp.exp2(scores - top)
                products = dot_nt(value, grad)
                total = jnp.sum(weights, axis=0, keepdims=True)
                center = jnp.sum(weights * products, axis=0, keepdims=True) / total
                return top + jnp.log2(total), center

            log_part, center = local(q_ref[:, columns(g, h)], do_ref[:, columns(g, h)], True)
            own_stat[g, pl.ds(h, 1), :] = log_part
            own_stat[g, pl.ds(heads + h, 1), :] = center
            for j in range(tiles):
                log_part, center = local(routed(g, j, 0, h), routed(g, j, 1, h), False)
                for half in range(2):
                    lanes = slice(half * LANES, (half + 1) * LANES)
                    stat_blk[g, 2 * j + half, pl.ds(h, 1), :] = log_part[:, lanes]
                    stat_blk[g, 2 * j + half, pl.ds(heads + h, 1), :] = center[:, lanes]
            return carry

        lax.fori_loop(0, heads, head, 0)
        upper(lambda s: stat_copy(g, me, s).start())

    def totals(g):
        lower(lambda d: stat_copy(g, d, me).wait_recv())
        count = 2 * heads
        gathered = three_parts(jnp.concatenate([back_buf[g, d] for d in range(blocks)], axis=1))
        logs = [own_stat[g, :heads]]
        centers = [own_stat[g, heads:]]
        for r in range(select_ref.shape[0]):
            got = add_parts(dot_nn(gathered, select_ref[r]), count)
            logs.append(jnp.where(present_ref[r : r + 1, :] > 0, got[:heads], NEGATIVE))
            centers.append(got[heads:])
        top = functools.reduce(jnp.maximum, logs)
        total = sum(jnp.exp2(part - top) for part in logs)
        log_total = top + jnp.log2(total)
        centering = sum(jnp.exp2(part - top) * c for part, c in zip(logs, centers)) / total
        final = jnp.concatenate([log_total, centering], axis=0)
        fin_own[g] = final
        parts = three_parts(final)
        both = select_ref[0]
        for r in range(1, select_ref.shape[0]):
            both = both + select_ref[r]
        spread = add_parts(dot_nt(parts, both), count)
        for d in range(blocks):
            log_send[g, d] = spread[:, d * LANES : (d + 1) * LANES]
        lower(lambda d: log_copy(g, me, d).start())

    def gradients(g):
        upper(lambda s: log_copy(g, s, me).wait_recv())
        for b in range(slots // LANES):
            slot_stat[:, b * LANES : (b + 1) * LANES] = sum(
                log_recv[g, b * per_blk + i] for i in range(per_blk)
            )

        def head(h, carry):
            key = k_ref[:, columns(g, h)]
            value = v_ref[:, columns(g, h)]
            key_turned = key.T

            def local(query, grad, log_row, center, mask):
                scores = dot_nt(key, query) * scale2
                probs = jnp.exp2(scores - log_row)
                if mask:
                    probs = jnp.where(own_mask(), probs, 0.0)
                products = dot_nt(value, grad)
                mixed = (probs * (products - center)).astype(BF16)
                dv = dot_nn(probs.astype(BF16), grad)
                dk = dot_nn(mixed, query)
                dq = (dot_nn(key_turned, mixed) * scaling).T
                return dq, dk, dv

            dq, dk, dv = local(
                q_ref[:, columns(g, h)],
                do_ref[:, columns(g, h)],
                fin_own[g, pl.ds(h, 1), :],
                fin_own[g, pl.ds(heads + h, 1), :],
                True,
            )
            dq_own[:, columns(g, h)] = dq
            for j in range(tiles):
                lanes = slice(j * tile, (j + 1) * tile)
                dq, dk_new, dv_new = local(
                    routed(g, j, 0, h),
                    routed(g, j, 1, h),
                    slot_stat[pl.ds(h, 1), lanes],
                    slot_stat[pl.ds(heads + h, 1), lanes],
                    False,
                )
                dk = dk + dk_new
                dv = dv + dv_new
                ret_send[g, j * per_tile : (j + 1) * per_tile, :, inner(h)] = dq.astype(BF16).reshape(
                    per_tile, cap, HEAD_DIM
                )
            shape = (nx, 2, rows, HEAD_DIM)
            kv_part[g, 0, :, :, :, inner(h)] = (dk * scaling).astype(BF16).reshape(shape)
            kv_part[g, 1, :, :, :, inner(h)] = dv.astype(BF16).reshape(shape)
            return carry

        lax.fori_loop(0, heads, head, 0)
        upper(lambda s: ret_copy(g, me, s).start())
        sib_copy(g).start()

    def pair_sums(g):
        sib_copy(g).wait_recv()
        for o in range(1, nx):
            other = lax.rem(xpos + o, nx)
            pair_send[g, other] = (
                kv_part[g, :, other, core].astype(F32) + sib_recv[g, :, other].astype(F32)
            ).astype(BF16)
            pair_copy(g, xpos, other).start()

    def finish(g):
        cols = pl.ds(pl.multiple_of(g * width, width), width)
        total = kv_part[g, :, xpos, core].astype(F32) + sib_recv[g, :, xpos].astype(F32)
        for o in range(1, nx):
            other = lax.rem(xpos + o, nx)
            pair_copy(g, other, xpos).wait_recv()
            total = total + pair_recv[g, other].astype(F32)
        dk_out[:, cols] = total[0].astype(BF16)
        dv_out[:, cols] = total[1].astype(BF16)
        lower(lambda d: ret_copy(g, d, me).wait_recv())
        terms = dot_nn(pick_rows[...], ret_recv[g].reshape(slots, width))
        dq_out[:, cols] = (dq_own[:, cols] + terms).astype(BF16)

    def step(i, carry):
        @pl.when((i >= 1) & (i < groups + 1))
        def _():
            totals(i - 1)

        @pl.when(i < groups)
        def _():
            statistics(i)

        @pl.when((i >= 1) & (i < groups + 1))
        def _():
            gradients(i - 1)

        @pl.when((i >= 2) & (i < groups + 2))
        def _():
            pair_sums(i - 2)

        @pl.when(i >= 3)
        def _():
            finish(i - 3)

        return carry

    lax.fori_loop(0, groups + 3, step, 0)

    def drain(g, carry):
        lower(lambda d: fwd_copy(g, me, d).wait_send())
        upper(lambda s: stat_copy(g, me, s).wait_send())
        lower(lambda d: log_copy(g, me, d).wait_send())
        upper(lambda s: ret_copy(g, me, s).wait_send())
        sib_copy(g).wait_send()
        for o in range(1, nx):
            pair_copy(g, xpos, lax.rem(xpos + o, nx)).wait_send()
        return carry

    lax.fori_loop(0, groups, drain, 0)


def per_device(blocks, helpers, query_rows, key_rows, value_rows, output_grad, block_choice):
    me = lax.axis_index("ctx")
    rows, features = query_rows.shape[1:]
    routes = block_choice.shape[2]
    keys = key_rows.shape[1]
    cap = max(16, 2 * max(1, rows // blocks))
    slots = blocks * cap
    width = min(GROUP_HEADS * HEAD_DIM, features)
    groups = features // width
    heads = width // HEAD_DIM
    nx = helpers // 2

    choice = block_choice[0].T
    present = choice < me
    targets = jnp.where(present, me - 1 - choice, -1)
    matches = (targets[:, None, :] == jnp.arange(blocks, dtype=jnp.int32)[None, :, None]).astype(jnp.int32)
    counts = jnp.sum(matches, axis=0)
    upto = (
        jnp.arange(rows, dtype=jnp.int32)[:, None] < jnp.arange(rows, dtype=jnp.int32)[None, :]
    ).astype(BF16)
    earlier = jnp.dot(counts.astype(BF16), upto, preferred_element_type=F32).astype(jnp.int32)
    places = jnp.sum(matches * earlier[None], axis=1)
    slot_ids = jnp.where(present, targets * cap + places, -1)
    slot_iota = jnp.arange(slots, dtype=jnp.int32)
    pick_slots = jnp.any(slot_ids[:, None, :] == slot_iota[None, :, None], axis=0).astype(BF16)
    pick_rows = jnp.any(slot_ids[:, :, None] == slot_iota[None, None, :], axis=0).astype(BF16)
    lane_ids = jnp.where(present, targets * LANES + lax.rem(me * cap, LANES) + places, -1)
    select = (lane_ids[:, None, :] == jnp.arange(blocks * LANES, dtype=jnp.int32)[None, :, None]).astype(BF16)

    count = 2 * heads
    dma = pltpu.SemaphoreType.DMA
    vmem = pl.BlockSpec(memory_space=pltpu.VMEM)
    out = jax.ShapeDtypeStruct((rows, features), BF16)
    dq, dk, dv = pl.pallas_call(
        functools.partial(kernel, blocks, helpers),
        out_shape=(out, out, out),
        in_specs=[vmem] * 8,
        out_specs=(vmem, vmem, vmem),
        scratch_shapes=[
            pltpu.VMEM((groups, blocks, 2, cap, width), BF16),
            pltpu.VMEM((groups, blocks, 2, cap, width), BF16),
            pltpu.VMEM((groups, count, rows), F32),
            pltpu.VMEM((groups, slots // LANES, count, LANES), F32),
            pltpu.VMEM((groups, blocks, count, LANES), F32),
            pltpu.VMEM((groups, blocks, count, LANES), F32),
            pltpu.VMEM((groups, blocks, count, LANES), F32),
            pltpu.VMEM((groups, count, rows), F32),
            pltpu.VMEM((count, slots), F32),
            pltpu.VMEM((rows, features), F32),
            pltpu.VMEM((groups, blocks, cap, width), BF16),
            pltpu.VMEM((groups, blocks, cap, width), BF16),
            pltpu.VMEM((groups, 2, nx, 2, rows, width), BF16),
            pltpu.VMEM((groups, 2, nx, rows, width), BF16),
            pltpu.VMEM((groups, nx, 2, rows, width), BF16),
            pltpu.VMEM((groups, nx, 2, rows, width), BF16),
        ]
        + [dma((groups, blocks))] * 8
        + [dma((groups,))] * 2
        + [dma((groups, nx))] * 2,
        compiler_params=pltpu.CompilerParams(
            collective_id=0, has_side_effects=True, vmem_limit_bytes=60 * 1024 * 1024
        ),
        name="routed_attention_grad",
    )(
        query_rows[0],
        key_rows[0],
        value_rows[0],
        output_grad[0],
        pick_slots,
        pick_rows,
        select,
        present.astype(jnp.int32),
    )
    return dq[None], dk[None], dv[None]


def solution(mesh):
    rows = P(None, ("ctx", "help"), None)
    block = P(None, "ctx", None)
    return jax.shard_map(
        functools.partial(per_device, mesh.shape["ctx"], mesh.shape["help"]),
        mesh=mesh,
        in_specs=(rows, block, block, rows, rows),
        out_specs=(rows, rows, rows),
        check_vma=False,
    )
```

```python
import functools

import jax
import jax.numpy as jnp
from jax import lax
from jax.experimental import pallas as pl
from jax.experimental.pallas import tpu as pltpu
from jax.sharding import PartitionSpec as P

HEAD_DIM = 128
LANES = 128
GROUP_HEADS = 2
AHEAD = 2
NEGATIVE = -1e30
LOG2E = 1.4426950408889634
F32 = jnp.float32
BF16 = jnp.bfloat16


def dot_nt(left, right):
    return lax.dot_general(left, right, (((1,), (1,)), ((), ())), preferred_element_type=F32)


def dot_nn(left, right):
    return lax.dot_general(left, right, (((1,), (0,)), ((), ())), preferred_element_type=F32)


def three_parts(value):
    high = value.astype(BF16).astype(F32)
    rest = value - high
    middle = rest.astype(BF16).astype(F32)
    return jnp.concatenate([high, middle, rest - middle], axis=0).astype(BF16)


def add_parts(value, count):
    return value[:count] + value[count : 2 * count] + value[2 * count :]


def kernel(
    blocks,
    helpers,
    q_ref,
    k_ref,
    v_ref,
    do_ref,
    pick_slots,
    pick_rows,
    select_ref,
    present_ref,
    dq_out,
    dk_out,
    dv_out,
    send_buf,
    recv_buf,
    own_stat,
    stat_blk,
    back_buf,
    log_send,
    log_recv,
    fin_own,
    slot_stat,
    dq_own,
    ret_send,
    ret_recv,
    kv_part,
    sib_recv,
    pair_send,
    pair_recv,
    fwd_s,
    fwd_r,
    stat_s,
    stat_r,
    log_s,
    log_r,
    ret_s,
    ret_r,
    sib_s,
    sib_r,
    pair_s,
    pair_r,
):
    me = lax.axis_index("ctx")
    helper = lax.axis_index("help")
    core = lax.rem(helper, 2)
    xpos = lax.div(helper, 2)
    nx = helpers // 2
    groups = send_buf.shape[0]
    cap = send_buf.shape[3]
    width = send_buf.shape[4]
    heads = width // HEAD_DIM
    rows = q_ref.shape[0]
    keys = k_ref.shape[0]
    slots = blocks * cap
    per_blk = LANES // cap
    tile = 2 * LANES
    tiles = slots // tile
    scaling = HEAD_DIM**-0.5
    scale2 = scaling * LOG2E

    def fwd_copy(g, src, dst):
        return pltpu.make_async_remote_copy(
            send_buf.at[g, dst], recv_buf.at[g, src], fwd_s.at[g, dst], fwd_r.at[g, src],
            device_id={"ctx": dst}, device_id_type=pl.DeviceIdType.MESH,
        )

    def stat_copy(g, src, dst):
        return pltpu.make_async_remote_copy(
            stat_blk.at[g, lax.div(dst, per_blk)], back_buf.at[g, src], stat_s.at[g, dst], stat_r.at[g, src],
            device_id={"ctx": dst}, device_id_type=pl.DeviceIdType.MESH,
        )

    def log_copy(g, src, dst):
        return pltpu.make_async_remote_copy(
            log_send.at[g, dst], log_recv.at[g, src], log_s.at[g, dst], log_r.at[g, src],
            device_id={"ctx": dst}, device_id_type=pl.DeviceIdType.MESH,
        )

    def ret_copy(g, src, dst):
        return pltpu.make_async_remote_copy(
            ret_send.at[g, dst], ret_recv.at[g, src], ret_s.at[g, dst], ret_r.at[g, src],
            device_id={"ctx": dst}, device_id_type=pl.DeviceIdType.MESH,
        )

    def sib_copy(g):
        return pltpu.make_async_remote_copy(
            kv_part.at[g, :, :, 1 - core], sib_recv.at[g], sib_s.at[g], sib_r.at[g],
            device_id={"help": xpos * 2 + 1 - core}, device_id_type=pl.DeviceIdType.MESH,
        )

    def pair_copy(g, src, dst):
        return pltpu.make_async_remote_copy(
            pair_send.at[g, dst], pair_recv.at[g, src], pair_s.at[g, dst], pair_r.at[g, src],
            device_id={"help": dst * 2 + core}, device_id_type=pl.DeviceIdType.MESH,
        )

    def lower(body):
        lax.fori_loop(0, me, lambda i, c: (body(me - 1 - i), c)[1], 0)

    def upper(body):
        lax.fori_loop(me + 1, blocks, lambda i, c: (body(i), c)[1], 0)

    barrier = pltpu.get_barrier_semaphore()

    def greet_ctx(d):
        pl.semaphore_signal(barrier, inc=1, device_id={"ctx": d}, device_id_type=pl.DeviceIdType.MESH)

    lower(greet_ctx)
    upper(greet_ctx)
    pl.semaphore_signal(
        barrier, inc=1, device_id={"help": xpos * 2 + 1 - core}, device_id_type=pl.DeviceIdType.MESH
    )
    for o in range(1, nx):
        pl.semaphore_signal(
            barrier, inc=1, device_id={"help": lax.rem(xpos + o, nx) * 2 + core},
            device_id_type=pl.DeviceIdType.MESH,
        )
    pl.semaphore_wait(barrier, blocks - 1 + nx)

    def pack(g, carry):
        cols = pl.ds(pl.multiple_of(g * width, width), width)
        for which, ref in ((0, q_ref), (1, do_ref)):
            packed = dot_nn(pick_slots[...], ref[:, cols]).astype(BF16)
            send_buf[g, :, which] = packed.reshape(blocks, cap, width)
        lower(lambda d: fwd_copy(g, me, d).start())
        return carry

    lax.fori_loop(0, min(AHEAD, groups), pack, 0)

    def clear(d, carry):
        @pl.when(d <= me)
        def _():
            def each(g, c):
                recv_buf[g, d] = jnp.zeros(recv_buf.shape[2:], BF16)
                log_recv[g, d] = jnp.zeros(log_recv.shape[2:], F32)
                return c

            lax.fori_loop(0, groups, each, 0)

        @pl.when(d >= me)
        def _():
            def each(g, c):
                back_buf[g, d] = jnp.zeros(back_buf.shape[2:], F32)
                ret_recv[g, d] = jnp.zeros(ret_recv.shape[2:], BF16)
                return c

            lax.fori_loop(0, groups, each, 0)

        return carry

    lax.fori_loop(0, blocks, clear, 0)

    def own_mask():
        row_at = helper * rows + lax.broadcasted_iota(jnp.int32, (keys, rows), 1)
        return lax.broadcasted_iota(jnp.int32, (keys, rows), 0) <= row_at

    def columns(g, h):
        return pl.ds(pl.multiple_of(g * width + h * HEAD_DIM, HEAD_DIM), HEAD_DIM)

    def inner(h):
        return pl.ds(pl.multiple_of(h * HEAD_DIM, HEAD_DIM), HEAD_DIM)

    per_tile = tile // cap

    def routed(g, j, which, h):
        return recv_buf[g, j * per_tile : (j + 1) * per_tile, which, :, inner(h)].reshape(tile, HEAD_DIM)

    def statistics(g):
        upper(lambda s: fwd_copy(g, s, me).wait_recv())

        def head(h, carry):
            key = k_ref[:, columns(g, h)]
            value = v_ref[:, columns(g, h)]

            def local(query, grad, mask):
                scores = dot_nt(key, query) * scale2
                if mask:
                    scores = jnp.where(own_mask(), scores, NEGATIVE)
                top = jnp.max(scores, axis=0, keepdims=True)
                weights = jnp.exp2(scores - top)
                products = dot_nt(value, grad)
                total = jnp.sum(weights, axis=0, keepdims=True)
                center = jnp.sum(weights * products, axis=0, keepdims=True) / total
                return top + jnp.log2(total), center

            log_part, center = local(q_ref[:, columns(g, h)], do_ref[:, columns(g, h)], True)
            own_stat[g, pl.ds(h, 1), :] = log_part
            own_stat[g, pl.ds(heads + h, 1), :] = center
            for j in range(tiles):
                log_part, center = local(routed(g, j, 0, h), routed(g, j, 1, h), False)
                for half in range(2):
                    lanes = slice(half * LANES, (half + 1) * LANES)
                    stat_blk[g, 2 * j + half, pl.ds(h, 1), :] = log_part[:, lanes]
                    stat_blk[g, 2 * j + half, pl.ds(heads + h, 1), :] = center[:, lanes]
            return carry

        lax.fori_loop(0, heads, head, 0)
        upper(lambda s: stat_copy(g, me, s).start())

    def totals(g):
        lower(lambda d: stat_copy(g, d, me).wait_recv())
        count = 2 * heads
        gathered = three_parts(jnp.concatenate([back_buf[g, d] for d in range(blocks)], axis=1))
        logs = [own_stat[g, :heads]]
        centers = [own_stat[g, heads:]]
        for r in range(select_ref.shape[0]):
            got = add_parts(dot_nn(gathered, select_ref[r]), count)
            logs.append(jnp.where(present_ref[r : r + 1, :] > 0, got[:heads], NEGATIVE))
            centers.append(got[heads:])
        top = functools.reduce(jnp.maximum, logs)
        total = sum(jnp.exp2(part - top) for part in logs)
        log_total = top + jnp.log2(total)
        centering = sum(jnp.exp2(part - top) * c for part, c in zip(logs, centers)) / total
        final = jnp.concatenate([log_total, centering], axis=0)
        fin_own[g] = final
        parts = three_parts(final)
        both = select_ref[0]
        for r in range(1, select_ref.shape[0]):
            both = both + select_ref[r]
        spread = add_parts(dot_nt(parts, both), count)
        for d in range(blocks):
            log_send[g, d] = spread[:, d * LANES : (d + 1) * LANES]
        lower(lambda d: log_copy(g, me, d).start())

    def gradients(g):
        upper(lambda s: log_copy(g, s, me).wait_recv())
        for b in range(slots // LANES):
            slot_stat[:, b * LANES : (b + 1) * LANES] = sum(
                log_recv[g, b * per_blk + i] for i in range(per_blk)
            )

        def head(h, carry):
            key = k_ref[:, columns(g, h)]
            value = v_ref[:, columns(g, h)]
            key_turned = key.T

            def local(query, grad, log_row, center, mask):
                scores = dot_nt(key, query) * scale2
                probs = jnp.exp2(scores - log_row)
                if mask:
                    probs = jnp.where(own_mask(), probs, 0.0)
                products = dot_nt(value, grad)
                mixed = (probs * (products - center)).astype(BF16)
                dv = dot_nn(probs.astype(BF16), grad)
                dk = dot_nn(mixed, query)
                dq = (dot_nn(key_turned, mixed) * scaling).T
                return dq, dk, dv

            dq, dk, dv = local(
                q_ref[:, columns(g, h)],
                do_ref[:, columns(g, h)],
                fin_own[g, pl.ds(h, 1), :],
                fin_own[g, pl.ds(heads + h, 1), :],
                True,
            )
            dq_own[:, columns(g, h)] = dq
            for j in range(tiles):
                lanes = slice(j * tile, (j + 1) * tile)
                dq, dk_new, dv_new = local(
                    routed(g, j, 0, h),
                    routed(g, j, 1, h),
                    slot_stat[pl.ds(h, 1), lanes],
                    slot_stat[pl.ds(heads + h, 1), lanes],
                    False,
                )
                dk = dk + dk_new
                dv = dv + dv_new
                ret_send[g, j * per_tile : (j + 1) * per_tile, :, inner(h)] = dq.astype(BF16).reshape(
                    per_tile, cap, HEAD_DIM
                )
            shape = (nx, 2, rows, HEAD_DIM)
            kv_part[g, 0, :, :, :, inner(h)] = (dk * scaling).astype(BF16).reshape(shape)
            kv_part[g, 1, :, :, :, inner(h)] = dv.astype(BF16).reshape(shape)
            return carry

        lax.fori_loop(0, heads, head, 0)
        upper(lambda s: ret_copy(g, me, s).start())
        sib_copy(g).start()

    def pair_sums(g):
        sib_copy(g).wait_recv()
        for o in range(1, nx):
            other = lax.rem(xpos + o, nx)
            pair_send[g, other] = (
                kv_part[g, :, other, core].astype(F32) + sib_recv[g, :, other].astype(F32)
            ).astype(BF16)
            pair_copy(g, xpos, other).start()

    def finish(g):
        cols = pl.ds(pl.multiple_of(g * width, width), width)
        total = kv_part[g, :, xpos, core].astype(F32) + sib_recv[g, :, xpos].astype(F32)
        for o in range(1, nx):
            other = lax.rem(xpos + o, nx)
            pair_copy(g, other, xpos).wait_recv()
            total = total + pair_recv[g, other].astype(F32)
        dk_out[:, cols] = total[0].astype(BF16)
        dv_out[:, cols] = total[1].astype(BF16)
        lower(lambda d: ret_copy(g, d, me).wait_recv())
        terms = dot_nn(pick_rows[...], ret_recv[g].reshape(slots, width))
        dq_out[:, cols] = (dq_own[:, cols] + terms).astype(BF16)

    def step(i, carry):
        @pl.when((i >= 1) & (i < groups + 1))
        def _():
            totals(i - 1)

        @pl.when(i + AHEAD < groups)
        def _():
            pack(i + AHEAD, 0)

        @pl.when(i < groups)
        def _():
            statistics(i)

        @pl.when((i >= 1) & (i < groups + 1))
        def _():
            gradients(i - 1)

        @pl.when((i >= 2) & (i < groups + 2))
        def _():
            pair_sums(i - 2)

        @pl.when(i >= 3)
        def _():
            finish(i - 3)

        return carry

    lax.fori_loop(0, groups + 3, step, 0)

    def drain(g, carry):
        lower(lambda d: fwd_copy(g, me, d).wait_send())
        upper(lambda s: stat_copy(g, me, s).wait_send())
        lower(lambda d: log_copy(g, me, d).wait_send())
        upper(lambda s: ret_copy(g, me, s).wait_send())
        sib_copy(g).wait_send()
        for o in range(1, nx):
            pair_copy(g, xpos, lax.rem(xpos + o, nx)).wait_send()
        return carry

    lax.fori_loop(0, groups, drain, 0)


def per_device(blocks, helpers, query_rows, key_rows, value_rows, output_grad, block_choice):
    me = lax.axis_index("ctx")
    rows, features = query_rows.shape[1:]
    routes = block_choice.shape[2]
    keys = key_rows.shape[1]
    cap = max(16, 2 * max(1, rows // blocks))
    slots = blocks * cap
    width = min(GROUP_HEADS * HEAD_DIM, features)
    groups = features // width
    heads = width // HEAD_DIM
    nx = helpers // 2

    choice = block_choice[0].T
    present = choice < me
    targets = jnp.where(present, me - 1 - choice, -1)
    matches = (targets[:, None, :] == jnp.arange(blocks, dtype=jnp.int32)[None, :, None]).astype(jnp.int32)
    counts = jnp.sum(matches, axis=0)
    upto = (
        jnp.arange(rows, dtype=jnp.int32)[:, None] < jnp.arange(rows, dtype=jnp.int32)[None, :]
    ).astype(BF16)
    earlier = jnp.dot(counts.astype(BF16), upto, preferred_element_type=F32).astype(jnp.int32)
    places = jnp.sum(matches * earlier[None], axis=1)
    slot_ids = jnp.where(present, targets * cap + places, -1)
    slot_iota = jnp.arange(slots, dtype=jnp.int32)
    pick_slots = jnp.any(slot_ids[:, None, :] == slot_iota[None, :, None], axis=0).astype(BF16)
    pick_rows = jnp.any(slot_ids[:, :, None] == slot_iota[None, None, :], axis=0).astype(BF16)
    lane_ids = jnp.where(present, targets * LANES + lax.rem(me * cap, LANES) + places, -1)
    select = (lane_ids[:, None, :] == jnp.arange(blocks * LANES, dtype=jnp.int32)[None, :, None]).astype(BF16)

    count = 2 * heads
    dma = pltpu.SemaphoreType.DMA
    vmem = pl.BlockSpec(memory_space=pltpu.VMEM)
    out = jax.ShapeDtypeStruct((rows, features), BF16)
    dq, dk, dv = pl.pallas_call(
        functools.partial(kernel, blocks, helpers),
        out_shape=(out, out, out),
        in_specs=[vmem] * 8,
        out_specs=(vmem, vmem, vmem),
        scratch_shapes=[
            pltpu.VMEM((groups, blocks, 2, cap, width), BF16),
            pltpu.VMEM((groups, blocks, 2, cap, width), BF16),
            pltpu.VMEM((groups, count, rows), F32),
            pltpu.VMEM((groups, slots // LANES, count, LANES), F32),
            pltpu.VMEM((groups, blocks, count, LANES), F32),
            pltpu.VMEM((groups, blocks, count, LANES), F32),
            pltpu.VMEM((groups, blocks, count, LANES), F32),
            pltpu.VMEM((groups, count, rows), F32),
            pltpu.VMEM((count, slots), F32),
            pltpu.VMEM((rows, features), F32),
            pltpu.VMEM((groups, blocks, cap, width), BF16),
            pltpu.VMEM((groups, blocks, cap, width), BF16),
            pltpu.VMEM((groups, 2, nx, 2, rows, width), BF16),
            pltpu.VMEM((groups, 2, nx, rows, width), BF16),
            pltpu.VMEM((groups, nx, 2, rows, width), BF16),
            pltpu.VMEM((groups, nx, 2, rows, width), BF16),
        ]
        + [dma((groups, blocks))] * 8
        + [dma((groups,))] * 2
        + [dma((groups, nx))] * 2,
        compiler_params=pltpu.CompilerParams(
            collective_id=0, has_side_effects=True, vmem_limit_bytes=60 * 1024 * 1024
        ),
        name="routed_attention_grad",
    )(
        query_rows[0],
        key_rows[0],
        value_rows[0],
        output_grad[0],
        pick_slots,
        pick_rows,
        select,
        present.astype(jnp.int32),
    )
    return dq[None], dk[None], dv[None]


def solution(mesh):
    rows = P(None, ("ctx", "help"), None)
    block = P(None, "ctx", None)
    return jax.shard_map(
        functools.partial(per_device, mesh.shape["ctx"], mesh.shape["help"]),
        mesh=mesh,
        in_specs=(rows, block, block, rows, rows),
        out_specs=(rows, rows, rows),
        check_vma=False,
    )
```

```python
import functools

import jax
import jax.numpy as jnp
from jax import lax
from jax.experimental import pallas as pl
from jax.experimental.pallas import tpu as pltpu
from jax.sharding import PartitionSpec as P

HEAD_DIM = 128
LANES = 128
GROUP_HEADS = 2
AHEAD = 1
NEGATIVE = -1e30
LOG2E = 1.4426950408889634
F32 = jnp.float32
BF16 = jnp.bfloat16


def dot_nt(left, right):
    return lax.dot_general(left, right, (((1,), (1,)), ((), ())), preferred_element_type=F32)


def dot_nn(left, right):
    return lax.dot_general(left, right, (((1,), (0,)), ((), ())), preferred_element_type=F32)


def three_parts(value):
    high = value.astype(BF16).astype(F32)
    rest = value - high
    middle = rest.astype(BF16).astype(F32)
    return jnp.concatenate([high, middle, rest - middle], axis=0).astype(BF16)


def add_parts(value, count):
    return value[:count] + value[count : 2 * count] + value[2 * count :]


def kernel(
    blocks,
    helpers,
    q_ref,
    k_ref,
    v_ref,
    do_ref,
    pick_slots,
    pick_rows,
    select_ref,
    present_ref,
    dq_out,
    dk_out,
    dv_out,
    send_buf,
    recv_buf,
    own_stat,
    stat_blk,
    back_buf,
    log_send,
    log_recv,
    fin_own,
    slot_stat,
    dq_own,
    ret_send,
    ret_recv,
    kv_part,
    sib_recv,
    pair_send,
    pair_recv,
    fwd_s,
    fwd_r,
    stat_s,
    stat_r,
    log_s,
    log_r,
    ret_s,
    ret_r,
    sib_s,
    sib_r,
    pair_s,
    pair_r,
):
    me = lax.axis_index("ctx")
    helper = lax.axis_index("help")
    core = lax.rem(helper, 2)
    xpos = lax.div(helper, 2)
    nx = helpers // 2
    groups = send_buf.shape[0]
    cap = send_buf.shape[3]
    width = send_buf.shape[4]
    heads = width // HEAD_DIM
    rows = q_ref.shape[0]
    keys = k_ref.shape[0]
    slots = blocks * cap
    per_blk = LANES // cap
    tile = 2 * LANES
    tiles = slots // tile
    scaling = HEAD_DIM**-0.5
    scale2 = scaling * LOG2E

    def fwd_copy(g, src, dst):
        return pltpu.make_async_remote_copy(
            send_buf.at[g, dst], recv_buf.at[g, src], fwd_s.at[g, dst], fwd_r.at[g, src],
            device_id={"ctx": dst}, device_id_type=pl.DeviceIdType.MESH,
        )

    def stat_copy(g, src, dst):
        return pltpu.make_async_remote_copy(
            stat_blk.at[g, lax.div(dst, per_blk)], back_buf.at[g, src], stat_s.at[g, dst], stat_r.at[g, src],
            device_id={"ctx": dst}, device_id_type=pl.DeviceIdType.MESH,
        )

    def log_copy(g, src, dst):
        return pltpu.make_async_remote_copy(
            log_send.at[g, dst], log_recv.at[g, src], log_s.at[g, dst], log_r.at[g, src],
            device_id={"ctx": dst}, device_id_type=pl.DeviceIdType.MESH,
        )

    def ret_copy(g, src, dst):
        return pltpu.make_async_remote_copy(
            ret_send.at[g, dst], ret_recv.at[g, src], ret_s.at[g, dst], ret_r.at[g, src],
            device_id={"ctx": dst}, device_id_type=pl.DeviceIdType.MESH,
        )

    def sib_copy(g):
        return pltpu.make_async_remote_copy(
            kv_part.at[g, :, :, 1 - core], sib_recv.at[g], sib_s.at[g], sib_r.at[g],
            device_id={"help": xpos * 2 + 1 - core}, device_id_type=pl.DeviceIdType.MESH,
        )

    def pair_copy(g, src, dst):
        return pltpu.make_async_remote_copy(
            pair_send.at[g, dst], pair_recv.at[g, src], pair_s.at[g, dst], pair_r.at[g, src],
            device_id={"help": dst * 2 + core}, device_id_type=pl.DeviceIdType.MESH,
        )

    def lower(body):
        lax.fori_loop(0, me, lambda i, c: (body(me - 1 - i), c)[1], 0)

    def upper(body):
        lax.fori_loop(me + 1, blocks, lambda i, c: (body(i), c)[1], 0)

    barrier = pltpu.get_barrier_semaphore()

    def greet_ctx(d):
        pl.semaphore_signal(barrier, inc=1, device_id={"ctx": d}, device_id_type=pl.DeviceIdType.MESH)

    lower(greet_ctx)
    upper(greet_ctx)
    pl.semaphore_signal(
        barrier, inc=1, device_id={"help": xpos * 2 + 1 - core}, device_id_type=pl.DeviceIdType.MESH
    )
    for o in range(1, nx):
        pl.semaphore_signal(
            barrier, inc=1, device_id={"help": lax.rem(xpos + o, nx) * 2 + core},
            device_id_type=pl.DeviceIdType.MESH,
        )
    pl.semaphore_wait(barrier, blocks - 1 + nx)

    def pack(g, carry):
        cols = pl.ds(pl.multiple_of(g * width, width), width)
        for which, ref in ((0, q_ref), (1, do_ref)):
            packed = dot_nn(pick_slots[...], ref[:, cols]).astype(BF16)
            send_buf[g, :, which] = packed.reshape(blocks, cap, width)
        lower(lambda d: fwd_copy(g, me, d).start())
        return carry

    lax.fori_loop(0, min(AHEAD, groups), pack, 0)

    def clear(d, carry):
        @pl.when(d <= me)
        def _():
            def each(g, c):
                recv_buf[g, d] = jnp.zeros(recv_buf.shape[2:], BF16)
                log_recv[g, d] = jnp.zeros(log_recv.shape[2:], F32)
                return c

            lax.fori_loop(0, groups, each, 0)

        @pl.when(d >= me)
        def _():
            def each(g, c):
                back_buf[g, d] = jnp.zeros(back_buf.shape[2:], F32)
                ret_recv[g, d] = jnp.zeros(ret_recv.shape[2:], BF16)
                return c

            lax.fori_loop(0, groups, each, 0)

        return carry

    lax.fori_loop(0, blocks, clear, 0)

    def own_mask():
        row_at = helper * rows + lax.broadcasted_iota(jnp.int32, (keys, rows), 1)
        return lax.broadcasted_iota(jnp.int32, (keys, rows), 0) <= row_at

    def columns(g, h):
        return pl.ds(pl.multiple_of(g * width + h * HEAD_DIM, HEAD_DIM), HEAD_DIM)

    def inner(h):
        return pl.ds(pl.multiple_of(h * HEAD_DIM, HEAD_DIM), HEAD_DIM)

    per_tile = tile // cap

    def routed(g, j, which, h):
        return recv_buf[g, j * per_tile : (j + 1) * per_tile, which, :, inner(h)].reshape(tile, HEAD_DIM)

    def statistics(g):
        upper(lambda s: fwd_copy(g, s, me).wait_recv())

        def head(h, carry):
            key = k_ref[:, columns(g, h)]
            value = v_ref[:, columns(g, h)]

            def local(query, grad, mask):
                scores = dot_nt(key, query) * scale2
                if mask:
                    scores = jnp.where(own_mask(), scores, NEGATIVE)
                top = jnp.max(scores, axis=0, keepdims=True)
                weights = jnp.exp2(scores - top)
                products = dot_nt(value, grad)
                total = jnp.sum(weights, axis=0, keepdims=True)
                center = jnp.sum(weights * products, axis=0, keepdims=True) / total
                return top + jnp.log2(total), center

            log_part, center = local(q_ref[:, columns(g, h)], do_ref[:, columns(g, h)], True)
            own_stat[g, pl.ds(h, 1), :] = log_part
            own_stat[g, pl.ds(heads + h, 1), :] = center
            for j in range(tiles):
                log_part, center = local(routed(g, j, 0, h), routed(g, j, 1, h), False)
                for half in range(2):
                    lanes = slice(half * LANES, (half + 1) * LANES)
                    stat_blk[g, 2 * j + half, pl.ds(h, 1), :] = log_part[:, lanes]
                    stat_blk[g, 2 * j + half, pl.ds(heads + h, 1), :] = center[:, lanes]
            return carry

        lax.fori_loop(0, heads, head, 0)
        upper(lambda s: stat_copy(g, me, s).start())

    def totals(g):
        lower(lambda d: stat_copy(g, d, me).wait_recv())
        count = 2 * heads
        gathered = three_parts(jnp.concatenate([back_buf[g, d] for d in range(blocks)], axis=1))
        logs = [own_stat[g, :heads]]
        centers = [own_stat[g, heads:]]
        for r in range(select_ref.shape[0]):
            got = add_parts(dot_nn(gathered, select_ref[r]), count)
            logs.append(jnp.where(present_ref[r : r + 1, :] > 0, got[:heads], NEGATIVE))
            centers.append(got[heads:])
        top = functools.reduce(jnp.maximum, logs)
        total = sum(jnp.exp2(part - top) for part in logs)
        log_total = top + jnp.log2(total)
        centering = sum(jnp.exp2(part - top) * c for part, c in zip(logs, centers)) / total
        final = jnp.concatenate([log_total, centering], axis=0)
        fin_own[g] = final
        parts = three_parts(final)
        both = select_ref[0]
        for r in range(1, select_ref.shape[0]):
            both = both + select_ref[r]
        spread = add_parts(dot_nt(parts, both), count)
        for d in range(blocks):
            log_send[g, d] = spread[:, d * LANES : (d + 1) * LANES]
        lower(lambda d: log_copy(g, me, d).start())

    def gradients(g):
        upper(lambda s: log_copy(g, s, me).wait_recv())
        for b in range(slots // LANES):
            slot_stat[:, b * LANES : (b + 1) * LANES] = sum(
                log_recv[g, b * per_blk + i] for i in range(per_blk)
            )

        def head(h, carry):
            key = k_ref[:, columns(g, h)]
            value = v_ref[:, columns(g, h)]
            key_turned = key.T

            def local(query, grad, log_row, center, mask):
                scores = dot_nt(key, query) * scale2
                probs = jnp.exp2(scores - log_row)
                if mask:
                    probs = jnp.where(own_mask(), probs, 0.0)
                products = dot_nt(value, grad)
                mixed = (probs * (products - center)).astype(BF16)
                dv = dot_nn(probs.astype(BF16), grad)
                dk = dot_nn(mixed, query)
                dq = (dot_nn(key_turned, mixed) * scaling).T
                return dq, dk, dv

            dq, dk, dv = local(
                q_ref[:, columns(g, h)],
                do_ref[:, columns(g, h)],
                fin_own[g, pl.ds(h, 1), :],
                fin_own[g, pl.ds(heads + h, 1), :],
                True,
            )
            dq_own[:, columns(g, h)] = dq
            for j in range(tiles):
                lanes = slice(j * tile, (j + 1) * tile)
                dq, dk_new, dv_new = local(
                    routed(g, j, 0, h),
                    routed(g, j, 1, h),
                    slot_stat[pl.ds(h, 1), lanes],
                    slot_stat[pl.ds(heads + h, 1), lanes],
                    False,
                )
                dk = dk + dk_new
                dv = dv + dv_new
                ret_send[g, j * per_tile : (j + 1) * per_tile, :, inner(h)] = dq.astype(BF16).reshape(
                    per_tile, cap, HEAD_DIM
                )
            shape = (nx, 2, rows, HEAD_DIM)
            kv_part[g, 0, :, :, :, inner(h)] = (dk * scaling).astype(BF16).reshape(shape)
            kv_part[g, 1, :, :, :, inner(h)] = dv.astype(BF16).reshape(shape)
            return carry

        lax.fori_loop(0, heads, head, 0)
        upper(lambda s: ret_copy(g, me, s).start())
        sib_copy(g).start()

    def pair_sums(g):
        sib_copy(g).wait_recv()
        for o in range(1, nx):
            other = lax.rem(xpos + o, nx)
            pair_send[g, other] = (
                kv_part[g, :, other, core].astype(F32) + sib_recv[g, :, other].astype(F32)
            ).astype(BF16)
            pair_copy(g, xpos, other).start()

    def finish(g):
        cols = pl.ds(pl.multiple_of(g * width, width), width)
        total = kv_part[g, :, xpos, core].astype(F32) + sib_recv[g, :, xpos].astype(F32)
        for o in range(1, nx):
            other = lax.rem(xpos + o, nx)
            pair_copy(g, other, xpos).wait_recv()
            total = total + pair_recv[g, other].astype(F32)
        dk_out[:, cols] = total[0].astype(BF16)
        dv_out[:, cols] = total[1].astype(BF16)
        lower(lambda d: ret_copy(g, d, me).wait_recv())
        terms = dot_nn(pick_rows[...], ret_recv[g].reshape(slots, width))
        dq_out[:, cols] = (dq_own[:, cols] + terms).astype(BF16)

    def step(i, carry):
        @pl.when((i >= 1) & (i < groups + 1))
        def _():
            totals(i - 1)

        @pl.when(i + AHEAD < groups)
        def _():
            pack(i + AHEAD, 0)

        @pl.when(i < groups)
        def _():
            statistics(i)

        @pl.when((i >= 1) & (i < groups + 1))
        def _():
            gradients(i - 1)

        @pl.when((i >= 2) & (i < groups + 2))
        def _():
            pair_sums(i - 2)

        @pl.when(i >= 3)
        def _():
            finish(i - 3)

        return carry

    lax.fori_loop(0, groups + 3, step, 0)

    def drain(g, carry):
        lower(lambda d: fwd_copy(g, me, d).wait_send())
        upper(lambda s: stat_copy(g, me, s).wait_send())
        lower(lambda d: log_copy(g, me, d).wait_send())
        upper(lambda s: ret_copy(g, me, s).wait_send())
        sib_copy(g).wait_send()
        for o in range(1, nx):
            pair_copy(g, xpos, lax.rem(xpos + o, nx)).wait_send()
        return carry

    lax.fori_loop(0, groups, drain, 0)


def per_device(blocks, helpers, query_rows, key_rows, value_rows, output_grad, block_choice):
    me = lax.axis_index("ctx")
    rows, features = query_rows.shape[1:]
    routes = block_choice.shape[2]
    keys = key_rows.shape[1]
    cap = max(16, 2 * max(1, rows // blocks))
    slots = blocks * cap
    width = min(GROUP_HEADS * HEAD_DIM, features)
    groups = features // width
    heads = width // HEAD_DIM
    nx = helpers // 2

    choice = block_choice[0].T
    present = choice < me
    targets = jnp.where(present, me - 1 - choice, -1)
    matches = (targets[:, None, :] == jnp.arange(blocks, dtype=jnp.int32)[None, :, None]).astype(jnp.int32)
    counts = jnp.sum(matches, axis=0)
    upto = (
        jnp.arange(rows, dtype=jnp.int32)[:, None] < jnp.arange(rows, dtype=jnp.int32)[None, :]
    ).astype(BF16)
    earlier = jnp.dot(counts.astype(BF16), upto, preferred_element_type=F32).astype(jnp.int32)
    places = jnp.sum(matches * earlier[None], axis=1)
    slot_ids = jnp.where(present, targets * cap + places, -1)
    slot_iota = jnp.arange(slots, dtype=jnp.int32)
    pick_slots = jnp.any(slot_ids[:, None, :] == slot_iota[None, :, None], axis=0).astype(BF16)
    pick_rows = jnp.any(slot_ids[:, :, None] == slot_iota[None, None, :], axis=0).astype(BF16)
    lane_ids = jnp.where(present, targets * LANES + lax.rem(me * cap, LANES) + places, -1)
    select = (lane_ids[:, None, :] == jnp.arange(blocks * LANES, dtype=jnp.int32)[None, :, None]).astype(BF16)

    count = 2 * heads
    dma = pltpu.SemaphoreType.DMA
    vmem = pl.BlockSpec(memory_space=pltpu.VMEM)
    out = jax.ShapeDtypeStruct((rows, features), BF16)
    dq, dk, dv = pl.pallas_call(
        functools.partial(kernel, blocks, helpers),
        out_shape=(out, out, out),
        in_specs=[vmem] * 8,
        out_specs=(vmem, vmem, vmem),
        scratch_shapes=[
            pltpu.VMEM((groups, blocks, 2, cap, width), BF16),
            pltpu.VMEM((groups, blocks, 2, cap, width), BF16),
            pltpu.VMEM((groups, count, rows), F32),
            pltpu.VMEM((groups, slots // LANES, count, LANES), F32),
            pltpu.VMEM((groups, blocks, count, LANES), F32),
            pltpu.VMEM((groups, blocks, count, LANES), F32),
            pltpu.VMEM((groups, blocks, count, LANES), F32),
            pltpu.VMEM((groups, count, rows), F32),
            pltpu.VMEM((count, slots), F32),
            pltpu.VMEM((rows, features), F32),
            pltpu.VMEM((groups, blocks, cap, width), BF16),
            pltpu.VMEM((groups, blocks, cap, width), BF16),
            pltpu.VMEM((groups, 2, nx, 2, rows, width), BF16),
            pltpu.VMEM((groups, 2, nx, rows, width), BF16),
            pltpu.VMEM((groups, nx, 2, rows, width), BF16),
            pltpu.VMEM((groups, nx, 2, rows, width), BF16),
        ]
        + [dma((groups, blocks))] * 8
        + [dma((groups,))] * 2
        + [dma((groups, nx))] * 2,
        compiler_params=pltpu.CompilerParams(
            collective_id=0, has_side_effects=True, vmem_limit_bytes=60 * 1024 * 1024
        ),
        name="routed_attention_grad",
    )(
        query_rows[0],
        key_rows[0],
        value_rows[0],
        output_grad[0],
        pick_slots,
        pick_rows,
        select,
        present.astype(jnp.int32),
    )
    return dq[None], dk[None], dv[None]


def solution(mesh):
    rows = P(None, ("ctx", "help"), None)
    block = P(None, "ctx", None)
    return jax.shard_map(
        functools.partial(per_device, mesh.shape["ctx"], mesh.shape["help"]),
        mesh=mesh,
        in_specs=(rows, block, block, rows, rows),
        out_specs=(rows, rows, rows),
        check_vma=False,
    )
```
